32 devices in a mesh: section: 4 (over z), seq: 8 (over y, x, core).
Axes of the slice: x: 2, y: 2, z: 4, core: 2. Of those that a mesh axis runs over, the one named last changes fastest.
Arguments:
- projected: bfloat16 [4, 3, 4096, 3072], P('section', None, 'seq'), may hold values from -24 to 24
- gate: bfloat16 [4, 3072], P('section'), may hold values from 2 to 8
- head_class: int32 [24], replicated, may hold values 0 or 1
- tile_lists: int32 [2, 32, 8], replicated, may hold values from 0 to 31, as said below
- tile_counts: int32 [24, 32], replicated, may hold values from 1 to 8, as said below
Outputs:
- next_input: bfloat16 [4, 4096, 3072], P('section', 'seq')
The draws below stay inside these ranges and needn't reach their ends.
Inputs may be any that keep to these rules, and one draw needn't show every extreme that they name: tile_lists[c, t, 0] = t, and the 8 entries of a row are distinct tiles. `tile_counts`: counts differ strongly from head to head.
All inputs are finite; a program needn't handle non-finite values.
Results may differ from the reference program's by a relative error of at most 0.0057.
Values may be sent and summed in bfloat16 or wider, within the bound.
A program may use at most 128 MiB of HBM per device.

```python
import jax
import jax.numpy as jnp
from jax import lax

H = 24
HD = 128
D = 3072
KMAX = 8
QG = 8
MICRO = 4
TOKENS = 4096
NT = 32
FT = 4
WIN = 15


def draw_projected(key, part):
    key = jax.random.fold_in(key, 11)
    base_key = jax.random.fold_in(key, 0)
    factors = jnp.array([1.7, 1.7, 1.0], jnp.float32)[None, :, None, None]
    fields = jax.random.normal(base_key, (MICRO, 3, TOKENS, D), jnp.float32) * factors
    return jnp.clip(fields, -24.0, 24.0).astype(jnp.bfloat16)


def draw_tile_lists(key, part):
    key = jax.random.fold_in(key, 23)
    near_key, far_key = jax.random.split(key)
    positions = jnp.arange(NT, dtype=jnp.int32)[:, None]
    near = jax.vmap(lambda subkey: jax.random.permutation(subkey, WIN))(jax.random.split(near_key, NT))
    near = near[:, :KMAX - 1].astype(jnp.int32) + 1
    far = jax.vmap(lambda subkey: jax.random.permutation(subkey, KMAX - 1))(jax.random.split(far_key, NT))
    far = (far.astype(jnp.int32) + 1) * FT
    zero_col = jnp.zeros((NT, 1), jnp.int32)
    spatial = (positions + jnp.concatenate([zero_col, near], axis=1)) % NT
    temporal = (positions + jnp.concatenate([zero_col, far], axis=1)) % NT
    return jnp.stack([spatial, temporal]).astype(jnp.int32)


def draw_tile_counts(key, part):
    key = jax.random.fold_in(key, 37)
    order_key, count_key = jax.random.split(key)
    order = jax.random.permutation(order_key, H).astype(jnp.int32)
    caps = 1 + order * (KMAX - 1) // (H - 1)
    drawn = jax.random.randint(count_key, (H, NT), 1, caps[:, None] + 1)
    return jnp.where(jnp.arange(NT)[None, :] == 0, caps[:, None], drawn).astype(jnp.int32)


def place_ends(entries, rng, low, high):
    longest = entries.shape.index(max(entries.shape))
    spots = []
    for shift in (0, 1):
        where = [jax.random.randint(jax.random.fold_in(rng, axis), (), 0, length) for axis, length in enumerate(entries.shape)]
        where[longest] = (where[longest] + shift) % entries.shape[longest]
        spots.append(tuple(where))
    return entries.at[spots[0]].set(low).at[spots[1]].set(high)


def levels(own_key, extent, cuts, low, largest):
    factor_of = 1.0
    for position, blocks in cuts:
        draws = jax.random.uniform(jax.random.fold_in(jax.random.fold_in(own_key, 6), position), (blocks,), jnp.float32, low / len(cuts), largest / len(cuts))
        factor_of = factor_of * jnp.repeat(jnp.exp(draws), extent[position] // blocks).reshape((-1,) + (1,) * (len(extent) - 1 - position))
    return factor_of


def setup_inputs(seed: int = 0) -> dict:
    keys = jax.random.split(jax.random.key(seed), 6)
    projected = draw_projected(jax.random.fold_in(keys[5], 71), 0)
    gate = jnp.clip(2.0 + 6.0 * jax.random.uniform(keys[1], (MICRO, D), jnp.float32) ** levels(keys[1], (MICRO, D), ((0, 4),), -0.2, 0.2), 2.0, 8.0).astype(jnp.bfloat16)
    head_class = place_ends((jax.random.randint(keys[2], (H,), 0, 2) < 1).astype(jnp.int32), jax.random.fold_in(keys[2], 1), 0, 1)
    tile_lists = draw_tile_lists(jax.random.fold_in(keys[5], 71), 0)
    tile_counts = draw_tile_counts(jax.random.fold_in(keys[5], 71), 0)
    return {"projected": projected, "gate": gate, "head_class": head_class, "tile_lists": tile_lists, "tile_counts": tile_counts}


def attend_tiles(queries, key_rows, value_rows, tile_rows, counts):
    ntiles = tile_rows.shape[0]
    kmax = tile_rows.shape[1]
    depth = queries.shape[1]
    tile_len = queries.shape[0] // ntiles
    scale_factor = depth ** -0.5
    query_tiles = queries.reshape(ntiles, tile_len, depth)
    key_tiles = key_rows.reshape(ntiles, tile_len, depth)
    value_tiles = value_rows.reshape(ntiles, tile_len, depth)

    def one_group(group):
        offset = (group * QG).astype(jnp.int32)
        group_queries = lax.dynamic_slice_in_dim(query_tiles, offset, QG, 0)
        group_rows = lax.dynamic_slice_in_dim(tile_rows, offset, QG, 0)
        group_counts = lax.dynamic_slice_in_dim(counts, offset, QG, 0)
        gathered_keys = key_tiles[group_rows].reshape(QG, kmax * tile_len, depth)
        gathered_values = value_tiles[group_rows].reshape(QG, kmax * tile_len, depth)
        scores = jnp.einsum("qtd,qkd->qtk", group_queries.astype(jnp.float32), gathered_keys.astype(jnp.float32)) * scale_factor
        usable = jnp.arange(kmax, dtype=jnp.int32)[None, :] < group_counts[:, None]
        usable = jnp.repeat(usable, tile_len, axis=1)[:, None, :]
        scores = jnp.where(usable, scores, -jnp.inf)
        highest = jnp.max(scores, axis=-1, keepdims=True)
        raised = jnp.exp(scores - highest)
        weights = (raised / jnp.sum(raised, axis=-1, keepdims=True)).astype(jnp.bfloat16)
        mixed = jnp.einsum("qtk,qkd->qtd", weights.astype(jnp.float32), gathered_values.astype(jnp.float32))
        return mixed.astype(jnp.bfloat16)

    grouped = lax.map(one_group, jnp.arange(ntiles // QG, dtype=jnp.int32))
    return grouped.reshape(ntiles * tile_len, depth)


def reference(projected, gate, head_class, tile_lists, tile_counts):
    batches = projected.shape[0]
    per_head = projected.reshape(batches, 3, TOKENS, H, HD).transpose(0, 3, 1, 2, 4).reshape(batches * H, 3, TOKENS, HD)
    head_lists = jnp.tile(tile_lists[head_class], (batches, 1, 1))
    head_counts = jnp.tile(tile_counts, (batches, 1))

    def attend_member(member):
        fields, tile_rows, counts = member
        return attend_tiles(fields[0], fields[1], fields[2], tile_rows, counts)

    results = lax.map(attend_member, (per_head, head_lists, head_counts))
    attended = results.reshape(batches, H, TOKENS, HD).transpose(0, 2, 1, 3).reshape(batches, TOKENS, H * HD)
    gated = (gate.astype(jnp.float32)[:, None, :] * attended.astype(jnp.float32)).astype(jnp.bfloat16)
    return jnp.roll(gated, 1, axis=0)
```

```python
import functools
import math

import jax
import jax.numpy as jnp
from jax import lax
from jax.experimental import pallas as pl
from jax.experimental.pallas import tpu as pltpu
from jax.sharding import PartitionSpec as P

HD = 128
MESH = pl.DeviceIdType.MESH


def relay_kernel(
    heads,
    owners,
    sections,
    slots,
    class_ref,
    lists_ref,
    counts_ref,
    gate_ref,
    fields_ref,
    out_ref,
    *scratch,
):
    members = scratch[:slots]
    staged = scratch[slots : 2 * slots]
    own_sem, in_send, in_recv, out_send, out_recv = scratch[2 * slots :]
    section = lax.axis_index("section")
    rank = lax.axis_index("seq")
    after = lax.rem(section + 1, sections)
    before = lax.rem(section + sections - 1, sections)
    chunk_tiles, tile_len = fields_ref.shape[1:3]
    local_len = chunk_tiles * tile_len
    kmax = lists_ref.shape[2]
    factor = HD ** (-0.5) * math.log2(math.e)
    valid = [min(owners, heads - slot * owners) for slot in range(slots)]

    def guarded(slot, member_rank, body):
        if valid[slot] == owners:
            body()
        else:
            pl.when(member_rank < valid[slot])(body)

    def columns(slot, member_rank):
        return pl.ds(pl.multiple_of((slot * owners + member_rank) * HD, HD), HD)

    def rows(member_rank):
        return pl.ds(pl.multiple_of(member_rank * local_len, local_len), local_len)

    def tiles(member_rank):
        return pl.ds(member_rank * chunk_tiles, chunk_tiles)

    def peer(distance):
        return lax.rem(rank + distance, owners)

    def in_copy(slot, target, source):
        return pltpu.make_async_remote_copy(
            src_ref=fields_ref.at[:, :, :, columns(slot, target)],
            dst_ref=members[slot].at[:, tiles(source)],
            send_sem=in_send.at[slot, target],
            recv_sem=in_recv.at[slot, source],
            device_id=(section, target),
            device_id_type=MESH,
        )

    def own_copy(slot):
        return pltpu.make_async_copy(
            fields_ref.at[:, :, :, columns(slot, rank)],
            members[slot].at[:, tiles(rank)],
            own_sem.at[slot],
        )

    def out_copy(slot, target, source):
        return pltpu.make_async_remote_copy(
            src_ref=staged[slot].at[rows(target), :],
            dst_ref=out_ref.at[:, columns(slot, source)],
            send_sem=out_send.at[slot, target],
            recv_sem=out_recv.at[slot, source],
            device_id=(after, target),
            device_id_type=MESH,
        )

    barrier = pltpu.get_barrier_semaphore()

    def greet_peer(distance, carry):
        pl.semaphore_signal(
            barrier, inc=1, device_id=(section, peer(distance)), device_id_type=MESH
        )
        return carry

    def greet_before(distance, carry):
        pl.semaphore_signal(
            barrier, inc=1, device_id=(before, peer(distance)), device_id_type=MESH
        )
        return carry

    lax.fori_loop(1, owners, greet_peer, 0)
    lax.fori_loop(0, owners, greet_before, 0)
    for slot in range(slots):
        guarded(slot, rank, lambda slot=slot: own_copy(slot).start())
    pl.semaphore_wait(barrier, 2 * owners - 1)

    def send_first(distance, carry):
        target = peer(distance)
        guarded(0, target, lambda: in_copy(0, target, rank).start())
        return carry

    lax.fori_loop(1, owners, send_first, 0)

    for slot in range(slots):
        if slot + 1 < slots:

            def send_next(distance, carry, slot=slot):
                target = peer(distance)
                guarded(slot, target, lambda: in_copy(slot, target, rank).wait_send())
                guarded(slot + 1, target, lambda: in_copy(slot + 1, target, rank).start())
                return carry

            lax.fori_loop(1, owners, send_next, 0)

        def attend_slot(slot=slot):
            own_copy(slot).wait()

            def receive(distance, carry):
                source = peer(distance)
                in_copy(slot, rank, source).wait_recv()
                return carry

            lax.fori_loop(1, owners, receive, 0)
            head = slot * owners + rank
            kind = class_ref[head]
            gate_part = gate_ref[:, pl.ds(pl.multiple_of(head * HD, HD), HD)].astype(jnp.float32)
            member = members[slot]

            def attend_tile(tile):
                here = pl.ds(pl.multiple_of(tile * tile_len, tile_len), tile_len)
                places = [
                    lists_ref[0, tile, j] + kind * (lists_ref[1, tile, j] - lists_ref[0, tile, j])
                    for j in range(kmax)
                ]
                queries = member[0, tile]
                keys = jnp.concatenate([member[1, place] for place in places], axis=0)
                values = jnp.concatenate([member[2, place] for place in places], axis=0)
                scores = lax.dot_general(
                    queries, keys, (((1,), (1,)), ((), ())), preferred_element_type=jnp.float32
                )
                index = lax.broadcasted_iota(jnp.int32, scores.shape, 1)
                scores = jnp.where(index < counts_ref[head, tile] * tile_len, scores, -jnp.inf)
                highest = jnp.max(scores, axis=-1, keepdims=True)
                raised = jnp.exp2((scores - highest) * factor)
                total = jnp.sum(raised, axis=-1, keepdims=True)
                weights = (raised * (1.0 / total)).astype(jnp.bfloat16)
                mixed = jnp.dot(weights, values, preferred_element_type=jnp.float32)
                mixed = mixed.astype(jnp.bfloat16).astype(jnp.float32)
                staged[slot][here, :] = (gate_part * mixed).astype(jnp.bfloat16)

            def attend_chunk(distance, carry):
                target = peer(distance)

                def step(i, inner):
                    attend_tile(target * chunk_tiles + 2 * i)
                    attend_tile(target * chunk_tiles + 2 * i + 1)
                    return inner

                if chunk_tiles % 2 == 0:
                    lax.fori_loop(0, chunk_tiles // 2, step, 0)
                else:
                    for i in range(chunk_tiles):
                        attend_tile(target * chunk_tiles + i)
                out_copy(slot, target, rank).start()
                return carry

            lax.fori_loop(0, owners, attend_chunk, 0)

        guarded(slot, rank, attend_slot)

    def finish_in(distance, carry):
        target = peer(distance)
        guarded(slots - 1, target, lambda: in_copy(slots - 1, target, rank).wait_send())
        return carry

    lax.fori_loop(1, owners, finish_in, 0)
    for slot in range(slots):

        def finish_send(slot=slot):
            def one(target, carry):
                out_copy(slot, target, rank).wait_send()
                return carry

            lax.fori_loop(0, owners, one, 0)

        guarded(slot, rank, finish_send)

        def finish_recv(source, carry, slot=slot):
            out_copy(slot, rank, source).wait_recv()
            return carry

        lax.fori_loop(0, valid[slot], finish_recv, 0)


def local(sections, owners, projected, gate, head_class, tile_lists, tile_counts):
    local_len, width = projected.shape[2:]
    heads = width // HD
    slots = -(-heads // owners)
    tokens = owners * local_len
    ntiles, kmax = tile_lists.shape[1:]
    tile_len = tokens // ntiles
    fields = projected.reshape(3, local_len // tile_len, tile_len, width)
    flops = 4 * slots * ntiles * tile_len * kmax * tile_len * HD
    smem = pl.BlockSpec(memory_space=pltpu.SMEM)
    out = pl.pallas_call(
        functools.partial(relay_kernel, heads, owners, sections, slots),
        out_shape=jax.ShapeDtypeStruct((local_len, width), jnp.bfloat16),
        in_specs=[smem, smem, smem, pl.BlockSpec(memory_space=pltpu.VMEM), pl.BlockSpec(memory_space=pl.ANY)],
        out_specs=pl.BlockSpec(memory_space=pl.ANY),
        scratch_shapes=[pltpu.VMEM((3, ntiles, tile_len, HD), jnp.bfloat16)] * slots
        + [pltpu.VMEM((tokens, HD), jnp.bfloat16)] * slots
        + [
            pltpu.SemaphoreType.DMA((slots,)),
            pltpu.SemaphoreType.DMA((slots, owners)),
            pltpu.SemaphoreType.DMA((slots, owners)),
            pltpu.SemaphoreType.DMA((slots, owners)),
            pltpu.SemaphoreType.DMA((slots, owners)),
        ],
        compiler_params=pltpu.CompilerParams(
            collective_id=0, has_side_effects=True, vmem_limit_bytes=56 * 1024 * 1024
        ),
        cost_estimate=pl.CostEstimate(
            flops=flops, bytes_accessed=8 * local_len * width, transcendentals=flops // (4 * HD)
        ),
    )(head_class, tile_lists, tile_counts, gate, fields)
    return out[None]


def solution(mesh):
    placed = (P("section", None, "seq", None), P("section", None), P(), P(), P())
    return jax.shard_map(
        functools.partial(local, mesh.shape["section"], mesh.shape["seq"]),
        mesh=mesh,
        in_specs=placed,
        out_specs=P("section", "seq", None),
        check_vma=False,
    )
```

```python
import functools
import math

import jax
import jax.numpy as jnp
from jax import lax
from jax.experimental import pallas as pl
from jax.experimental.pallas import tpu as pltpu
from jax.sharding import PartitionSpec as P

HD = 128
MESH = pl.DeviceIdType.MESH


def relay_kernel(
    heads,
    owners,
    sections,
    slots,
    class_ref,
    lists_ref,
    counts_ref,
    gate_ref,
    fields_ref,
    out_ref,
    *scratch,
):
    queries = scratch[:slots]
    pairs = scratch[slots : 2 * slots]
    staged = scratch[2 * slots : 3 * slots]
    own_sem, q_send, q_recv, kv_send, kv_recv, out_send, out_recv = scratch[3 * slots :]
    section = lax.axis_index("section")
    rank = lax.axis_index("seq")
    after = lax.rem(section + 1, sections)
    before = lax.rem(section + sections - 1, sections)
    chunk_tiles, tile_len = fields_ref.shape[1:3]
    local_len = chunk_tiles * tile_len
    kmax = lists_ref.shape[1]
    factor = HD ** (-0.5) * math.log2(math.e)
    valid = [min(owners, heads - slot * owners) for slot in range(slots)]
    half = owners // 2

    def guarded(slot, member_rank, body):
        if valid[slot] == owners:
            body()
        else:
            pl.when(member_rank < valid[slot])(body)

    def columns(slot, member_rank):
        return pl.ds(pl.multiple_of((slot * owners + member_rank) * HD, HD), HD)

    def rows(member_rank):
        return pl.ds(pl.multiple_of(member_rank * local_len, local_len), local_len)

    def tiles(member_rank):
        return pl.ds(member_rank * chunk_tiles, chunk_tiles)

    def peer(step):
        distance = 2 * lax.rem(step, half) + lax.div(step, half)
        other = 0
        bit = 1
        while bit < owners:
            other = other + bit * lax.rem(lax.div(rank, bit) + lax.div(distance, bit), 2)
            bit *= 2
        return other

    def q_copy(slot, target, source):
        return pltpu.make_async_remote_copy(
            src_ref=fields_ref.at[0, :, :, columns(slot, target)],
            dst_ref=queries[slot].at[tiles(source)],
            send_sem=q_send.at[slot, target],
            recv_sem=q_recv.at[slot, source],
            device_id=(section, target),
            device_id_type=MESH,
        )

    def kv_copy(slot, target, source):
        return pltpu.make_async_remote_copy(
            src_ref=fields_ref.at[pl.ds(1, 2), :, :, columns(slot, target)],
            dst_ref=pairs[slot].at[:, tiles(source)],
            send_sem=kv_send.at[slot, target],
            recv_sem=kv_recv.at[slot, source],
            device_id=(section, target),
            device_id_type=MESH,
        )

    def own_q_copy(slot):
        return pltpu.make_async_copy(
            fields_ref.at[0, :, :, columns(slot, rank)],
            queries[slot].at[tiles(rank)],
            own_sem.at[slot, 0],
        )

    def own_kv_copy(slot):
        return pltpu.make_async_copy(
            fields_ref.at[pl.ds(1, 2), :, :, columns(slot, rank)],
            pairs[slot].at[:, tiles(rank)],
            own_sem.at[slot, 1],
        )

    def out_copy(slot, target, source):
        return pltpu.make_async_remote_copy(
            src_ref=staged[slot].at[rows(target), :],
            dst_ref=out_ref.at[:, columns(slot, source)],
            send_sem=out_send.at[slot, target],
            recv_sem=out_recv.at[slot, source],
            device_id=(after, target),
            device_id_type=MESH,
        )

    def each(first, last, body):
        def step(i, carry):
            body(peer(i))
            return carry

        lax.fori_loop(first, last, step, 0)

    def to_peers(slot, first, last, body):
        each(first, last, lambda target: guarded(slot, target, lambda: body(target)))

    barrier = pltpu.get_barrier_semaphore()

    def greet(place):
        def one(target):
            pl.semaphore_signal(barrier, inc=1, device_id=(place, target), device_id_type=MESH)

        return one

    each(1, owners, greet(section))
    each(0, owners, greet(before))

    def start_own(slot):
        own_q_copy(slot).start()
        own_kv_copy(slot).start()

    for slot in range(slots):
        guarded(slot, rank, functools.partial(start_own, slot))
    pl.semaphore_wait(barrier, 2 * owners - 1)

    to_peers(0, 1, owners, lambda target: kv_copy(0, target, rank).start())
    if slots > 1:
        to_peers(0, 1, owners, lambda target: q_copy(0, target, rank).start())

    for slot in range(slots):
        final = slot == slots - 1

        def kv_sent(target, slot=slot):
            kv_copy(slot, target, rank).wait_send()

        def q_start(target, slot=slot):
            q_copy(slot, target, rank).start()

        def q_sent(target, slot=slot):
            q_copy(slot, target, rank).wait_send()

        def gather_pairs(slot=slot):
            own_q_copy(slot).wait()
            own_kv_copy(slot).wait()
            each(1, owners, lambda source: kv_copy(slot, rank, source).wait_recv())

        def attend_chunks(first, last, slot=slot):
            head = slot * owners + rank
            kind = class_ref[head]
            gate_part = gate_ref[:, pl.ds(pl.multiple_of(head * HD, HD), HD)].astype(jnp.float32)

            def attend_tile(tile):
                here = pl.ds(pl.multiple_of(tile * tile_len, tile_len), tile_len)
                places = [
                    lists_ref[0, j, tile] + kind * (lists_ref[1, j, tile] - lists_ref[0, j, tile])
                    for j in range(kmax)
                ]
                keys = jnp.concatenate([pairs[slot][0, place] for place in places], axis=0)
                values = jnp.concatenate([pairs[slot][1, place] for place in places], axis=0)
                scores = lax.dot_general(
                    queries[slot][tile],
                    keys,
                    (((1,), (1,)), ((), ())),
                    preferred_element_type=jnp.float32,
                )
                index = lax.broadcasted_iota(jnp.int32, scores.shape, 1)
                scores = jnp.where(index < counts_ref[head, tile] * tile_len, scores, -jnp.inf)
                highest = jnp.max(scores, axis=-1, keepdims=True)
                raised = jnp.exp2((scores - highest) * factor)
                total = jnp.sum(raised, axis=-1, keepdims=True)
                weights = (raised * (1.0 / total)).astype(jnp.bfloat16)
                mixed = jnp.dot(weights, values, preferred_element_type=jnp.float32)
                mixed = mixed.astype(jnp.bfloat16).astype(jnp.float32)
                staged[slot][here, :] = (gate_part * mixed).astype(jnp.bfloat16)

            def attend_chunk(step, carry):
                target = peer(step)

                @pl.when(step > 0)
                def _():
                    q_copy(slot, rank, target).wait_recv()

                def attend_two(i, inner):
                    attend_tile(target * chunk_tiles + 2 * i)
                    attend_tile(target * chunk_tiles + 2 * i + 1)
                    return inner

                if chunk_tiles % 2 == 0:
                    lax.fori_loop(0, chunk_tiles // 2, attend_two, 0)
                else:
                    for i in range(chunk_tiles):
                        attend_tile(target * chunk_tiles + i)
                out_copy(slot, target, rank).start()
                return carry

            lax.fori_loop(first, last, attend_chunk, 0)

        if not final:

            def kv_next(target, slot=slot):
                guarded(slot, target, lambda: kv_copy(slot, target, rank).wait_send())
                guarded(slot + 1, target, lambda: kv_copy(slot + 1, target, rank).start())

            each(1, owners, kv_next)
            guarded(slot, rank, gather_pairs)
            guarded(slot, rank, functools.partial(attend_chunks, 0, owners))
            to_peers(slot, 1, owners, q_sent)
            if slot + 1 < slots - 1:
                to_peers(
                    slot + 1, 1, owners, lambda target: q_copy(slot + 1, target, rank).start()
                )
        else:

            def q_after_kv(target):
                kv_sent(target)
                q_start(target)

            to_peers(slot, 1, half, q_after_kv)
            guarded(slot, rank, gather_pairs)
            guarded(slot, rank, functools.partial(attend_chunks, 0, 1))
            to_peers(slot, 1, half, q_sent)
            to_peers(slot, half, owners, q_after_kv)
            guarded(slot, rank, functools.partial(attend_chunks, 1, owners))
            to_peers(slot, half, owners, q_sent)

    for slot in range(slots):

        def finish_send(slot=slot):
            each(0, owners, lambda target: out_copy(slot, target, rank).wait_send())

        guarded(slot, rank, finish_send)

        def finish_recv(source, carry, slot=slot):
            out_copy(slot, rank, source).wait_recv()
            return carry

        lax.fori_loop(0, valid[slot], finish_recv, 0)


def local(sections, owners, projected, gate, head_class, tile_lists, tile_counts):
    local_len, width = projected.shape[2:]
    heads = width // HD
    slots = -(-heads // owners)
    tokens = owners * local_len
    ntiles, kmax = tile_lists.shape[1:]
    tile_len = tokens // ntiles
    fields = projected.reshape(3, local_len // tile_len, tile_len, width)
    flops = 4 * slots * ntiles * tile_len * kmax * tile_len * HD
    smem = pl.BlockSpec(memory_space=pltpu.SMEM)
    out = pl.pallas_call(
        functools.partial(relay_kernel, heads, owners, sections, slots),
        out_shape=jax.ShapeDtypeStruct((local_len, width), jnp.bfloat16),
        in_specs=[smem, smem, smem, pl.BlockSpec(memory_space=pltpu.VMEM), pl.BlockSpec(memory_space=pl.ANY)],
        out_specs=pl.BlockSpec(memory_space=pl.ANY),
        scratch_shapes=[pltpu.VMEM((ntiles, tile_len, HD), jnp.bfloat16)] * slots
        + [pltpu.VMEM((2, ntiles, tile_len, HD), jnp.bfloat16)] * slots
        + [pltpu.VMEM((tokens, HD), jnp.bfloat16)] * slots
        + [
            pltpu.SemaphoreType.DMA((slots, 2)),
            pltpu.SemaphoreType.DMA((slots, owners)),
            pltpu.SemaphoreType.DMA((slots, owners)),
            pltpu.SemaphoreType.DMA((slots, owners)),
            pltpu.SemaphoreType.DMA((slots, owners)),
            pltpu.SemaphoreType.DMA((slots, owners)),
            pltpu.SemaphoreType.DMA((slots, owners)),
        ],
        compiler_params=pltpu.CompilerParams(
            collective_id=0, has_side_effects=True, vmem_limit_bytes=56 * 1024 * 1024
        ),
        cost_estimate=pl.CostEstimate(
            flops=flops, bytes_accessed=8 * local_len * width, transcendentals=flops // (4 * HD)
        ),
    )(head_class, tile_lists.transpose(0, 2, 1), tile_counts, gate, fields)
    return out[None]


def solution(mesh):
    placed = (P("section", None, "seq", None), P("section", None), P(), P(), P())
    return jax.shard_map(
        functools.partial(local, mesh.shape["section"], mesh.shape["seq"]),
        mesh=mesh,
        in_specs=placed,
        out_specs=P("section", "seq", None),
        check_vma=False,
    )
```

```python
import functools
import math

import jax
import jax.numpy as jnp
from jax import lax
from jax.experimental import pallas as pl
from jax.experimental.pallas import tpu as pltpu
from jax.sharding import PartitionSpec as P

HD = 128
MESH = pl.DeviceIdType.MESH


def relay_kernel(
    heads,
    owners,
    sections,
    slots,
    class_ref,
    lists_ref,
    counts_ref,
    gate_ref,
    fields_ref,
    out_ref,
    *scratch,
):
    queries = scratch[:slots]
    pairs = scratch[slots : 2 * slots]
    staged = scratch[2 * slots : 3 * slots]
    usable = scratch[3 * slots]
    own_sem, q_send, q_recv, kv_send, kv_recv, out_send, out_recv = scratch[3 * slots + 1 :]
    section = lax.axis_index("section")
    rank = lax.axis_index("seq")
    after = lax.rem(section + 1, sections)
    before = lax.rem(section + sections - 1, sections)
    chunk_tiles, tile_len = fields_ref.shape[1:3]
    local_len = chunk_tiles * tile_len
    kmax, ntiles = lists_ref.shape[1:]
    factor = HD ** (-0.5) * math.log2(math.e)
    valid = [min(owners, heads - slot * owners) for slot in range(slots)]
    half = owners // 2
    chip, core = lax.div(rank, 2), lax.rem(rank, 2)

    def guarded(slot, member_rank, body):
        if valid[slot] == owners:
            body()
        else:
            pl.when(member_rank < valid[slot])(body)

    def columns(slot, member_rank):
        return pl.ds(pl.multiple_of((slot * owners + member_rank) * HD, HD), HD)

    def rows(member_rank):
        return pl.ds(pl.multiple_of(member_rank * local_len, local_len), local_len)

    def tiles(member_rank):
        return pl.ds(member_rank * chunk_tiles, chunk_tiles)

    def flipped(index, distance):
        other = 0
        bit = 1
        while bit < half:
            other = other + bit * lax.rem(lax.div(index, bit) + lax.div(distance, bit), 2)
            bit *= 2
        return other

    def peer(step):
        return 2 * flipped(chip, lax.rem(step, half)) + lax.rem(core + lax.div(step, half), 2)

    def q_copy(slot, target, source):
        return pltpu.make_async_remote_copy(
            src_ref=fields_ref.at[0, :, :, columns(slot, target)],
            dst_ref=queries[slot].at[tiles(source)],
            send_sem=q_send.at[slot, target],
            recv_sem=q_recv.at[slot, source],
            device_id=(section, target),
            device_id_type=MESH,
        )

    def kv_copy(slot, target, source):
        return pltpu.make_async_remote_copy(
            src_ref=fields_ref.at[pl.ds(1, 2), :, :, columns(slot, target)],
            dst_ref=pairs[slot].at[:, tiles(source)],
            send_sem=kv_send.at[slot, target],
            recv_sem=kv_recv.at[slot, source],
            device_id=(section, target),
            device_id_type=MESH,
        )

    def own_q_copy(slot):
        return pltpu.make_async_copy(
            fields_ref.at[0, :, :, columns(slot, rank)],
            queries[slot].at[tiles(rank)],
            own_sem.at[slot, 0],
        )

    def own_kv_copy(slot):
        return pltpu.make_async_copy(
            fields_ref.at[pl.ds(1, 2), :, :, columns(slot, rank)],
            pairs[slot].at[:, tiles(rank)],
            own_sem.at[slot, 1],
        )

    def out_copy(slot, target, source):
        return pltpu.make_async_remote_copy(
            src_ref=staged[slot].at[rows(target), :],
            dst_ref=out_ref.at[:, columns(slot, source)],
            send_sem=out_send.at[slot, target],
            recv_sem=out_recv.at[slot, source],
            device_id=(after, target),
            device_id_type=MESH,
        )

    def each(first, last, body):
        def step(i, carry):
            body(peer(i))
            return carry

        lax.fori_loop(first, last, step, 0)

    def to_core(slot, side, body):
        def one(target):
            guarded(slot, target, lambda: body(target))

        pl.when(core != side)(lambda: one(2 * chip + side))

        def step(distance, carry):
            one(2 * flipped(chip, distance) + side)
            return carry

        lax.fori_loop(1, half, step, 0)

    def sent_then(copy, slot, side, following):
        def sent(distance):
            target = 2 * flipped(chip, distance) + side
            guarded(slot, target, lambda: copy(slot, target, rank).wait_send())

        def start(distance):
            target = 2 * flipped(chip, distance) + 1 - side
            guarded(following, target, lambda: copy(following, target, rank).start())

        pl.when(core != side)(lambda: sent(0))
        if following < slots:
            pl.when(core == side)(lambda: start(0))

        def step(distance, carry):
            sent(distance)
            if following < slots:
                start(distance)
            return carry

        lax.fori_loop(1, half, step, 0)

    usable[0] = jnp.zeros((tile_len, HD), jnp.bfloat16)
    usable[1] = jnp.ones((tile_len, HD), jnp.bfloat16)
    for slot in range(slots):
        pairs[slot][:, ntiles] = jnp.zeros((2, tile_len, HD), jnp.bfloat16)

    barrier = pltpu.get_barrier_semaphore()

    def greet(place):
        def one(target):
            pl.semaphore_signal(barrier, inc=1, device_id=(place, target), device_id_type=MESH)

        return one

    each(1, owners, greet(section))
    each(0, owners, greet(before))

    def start_own(slot):
        own_q_copy(slot).start()
        own_kv_copy(slot).start()

    for slot in range(slots):
        guarded(slot, rank, functools.partial(start_own, slot))
    pl.semaphore_wait(barrier, 2 * owners - 1)

    to_core(0, 0, lambda target: kv_copy(0, target, rank).start())
    to_core(0, 0, lambda target: q_copy(0, target, rank).start())

    for slot in range(slots):
        def gather_pairs(slot=slot):
            own_q_copy(slot).wait()
            own_kv_copy(slot).wait()
            each(1, owners, lambda source: kv_copy(slot, rank, source).wait_recv())

        def attend_chunks(first, last, slot=slot):
            head = slot * owners + rank
            kind = class_ref[head]
            gate_part = gate_ref[:, pl.ds(pl.multiple_of(head * HD, HD), HD)].astype(jnp.float32)

            def attend_tile(tile):
                here = pl.ds(pl.multiple_of(tile * tile_len, tile_len), tile_len)
                count = counts_ref[head, tile]
                places, fillers, flags = [tile], [tile], [1]
                for j in range(1, kmax):
                    listed = lists_ref[0, j, tile] + kind * (
                        lists_ref[1, j, tile] - lists_ref[0, j, tile]
                    )
                    places.append(jnp.where(j < count, listed, tile))
                    fillers.append(jnp.where(j < count, listed, ntiles))
                    flags.append(jnp.where(j < count, 1, 0))
                keys = jnp.concatenate([pairs[slot][0, place] for place in places], axis=0)
                values = jnp.concatenate([pairs[slot][1, place] for place in fillers], axis=0)
                marks = jnp.concatenate([usable[flag] for flag in flags], axis=0)
                values = jnp.concatenate([values, marks], axis=1)
                scores = lax.dot_general(
                    queries[slot][tile],
                    keys,
                    (((1,), (1,)), ((), ())),
                    preferred_element_type=jnp.float32,
                )
                highest = jnp.max(scores, axis=-1, keepdims=True)
                raised = jnp.exp2((scores - highest) * factor).astype(jnp.bfloat16)
                mixed = jnp.dot(raised, values, preferred_element_type=jnp.float32)
                mixed = mixed[:, :HD] / mixed[:, HD:]
                mixed = mixed.astype(jnp.bfloat16).astype(jnp.float32)
                staged[slot][here, :] = (gate_part * mixed).astype(jnp.bfloat16)

            def attend_chunk(step, carry):
                target = peer(step)

                @pl.when(step > 0)
                def _():
                    q_copy(slot, rank, target).wait_recv()

                def attend_two(i, inner):
                    attend_tile(target * chunk_tiles + 2 * i)
                    attend_tile(target * chunk_tiles + 2 * i + 1)
                    return inner

                if chunk_tiles % 2 == 0:
                    lax.fori_loop(0, chunk_tiles // 2, attend_two, 0)
                else:
                    for i in range(chunk_tiles):
                        attend_tile(target * chunk_tiles + i)
                out_copy(slot, target, rank).start()
                return carry

            lax.fori_loop(first, last, attend_chunk, 0)

        def attend_slot(slot=slot, attend_chunks=attend_chunks, gather_pairs=gather_pairs):
            gather_pairs()
            attend_chunks(0, owners)

        for side in range(2):
            following = slot + side
            for copy in (kv_copy, q_copy):
                sent_then(copy, slot, side, following)

            @pl.when(core == side)
            def _(slot=slot, attend_slot=attend_slot):
                guarded(slot, rank, attend_slot)

    for slot in range(slots):

        def finish_send(slot=slot):
            each(0, owners, lambda target: out_copy(slot, target, rank).wait_send())

        guarded(slot, rank, finish_send)

        def finish_recv(source, carry, slot=slot):
            out_copy(slot, rank, source).wait_recv()
            return carry

        lax.fori_loop(0, valid[slot], finish_recv, 0)


def local(sections, owners, projected, gate, head_class, tile_lists, tile_counts):
    local_len, width = projected.shape[2:]
    heads = width // HD
    slots = -(-heads // owners)
    tokens = owners * local_len
    ntiles, kmax = tile_lists.shape[1:]
    tile_len = tokens // ntiles
    fields = projected.reshape(3, local_len // tile_len, tile_len, width)
    flops = 4 * slots * ntiles * tile_len * kmax * tile_len * HD
    smem = pl.BlockSpec(memory_space=pltpu.SMEM)
    out = pl.pallas_call(
        functools.partial(relay_kernel, heads, owners, sections, slots),
        out_shape=jax.ShapeDtypeStruct((local_len, width), jnp.bfloat16),
        in_specs=[smem, smem, smem, pl.BlockSpec(memory_space=pltpu.VMEM), pl.BlockSpec(memory_space=pl.ANY)],
        out_specs=pl.BlockSpec(memory_space=pl.ANY),
        scratch_shapes=[pltpu.VMEM((ntiles, tile_len, HD), jnp.bfloat16)] * slots
        + [pltpu.VMEM((2, ntiles + 1, tile_len, HD), jnp.bfloat16)] * slots
        + [pltpu.VMEM((tokens, HD), jnp.bfloat16)] * slots
        + [pltpu.VMEM((2, tile_len, HD), jnp.bfloat16)]
        + [
            pltpu.SemaphoreType.DMA((slots, 2)),
            pltpu.SemaphoreType.DMA((slots, owners)),
            pltpu.SemaphoreType.DMA((slots, owners)),
            pltpu.SemaphoreType.DMA((slots, owners)),
            pltpu.SemaphoreType.DMA((slots, owners)),
            pltpu.SemaphoreType.DMA((slots, owners)),
            pltpu.SemaphoreType.DMA((slots, owners)),
        ],
        compiler_params=pltpu.CompilerParams(
            collective_id=0, has_side_effects=True, vmem_limit_bytes=56 * 1024 * 1024
        ),
        cost_estimate=pl.CostEstimate(
            flops=flops, bytes_accessed=8 * local_len * width, transcendentals=flops // (4 * HD)
        ),
    )(head_class, tile_lists.transpose(0, 2, 1), tile_counts, gate, fields)
    return out[None]


def solution(mesh):
    placed = (P("section", None, "seq", None), P("section", None), P(), P(), P())
    return jax.shard_map(
        functools.partial(local, mesh.shape["section"], mesh.shape["seq"]),
        mesh=mesh,
        in_specs=placed,
        out_specs=P("section", "seq", None),
        check_vma=False,
    )
```

```python
import functools
import math

import jax
import jax.numpy as jnp
from jax import lax
from jax.experimental import pallas as pl
from jax.experimental.pallas import tpu as pltpu
from jax.sharding import PartitionSpec as P

HD = 128
MESH = pl.DeviceIdType.MESH


def relay_kernel(
    heads,
    owners,
    sections,
    slots,
    class_ref,
    lists_ref,
    counts_ref,
    gate_ref,
    fields_ref,
    out_ref,
    *scratch,
):
    queries = scratch[:slots]
    pairs = scratch[slots : 2 * slots]
    staged = scratch[2 * slots : 3 * slots]
    usable = scratch[3 * slots]
    own_sem, q_send, q_recv, kv_send, kv_recv, out_send, out_recv = scratch[3 * slots + 1 :]
    section = lax.axis_index("section")
    rank = lax.axis_index("seq")
    after = lax.rem(section + 1, sections)
    before = lax.rem(section + sections - 1, sections)
    chunk_tiles, tile_len = fields_ref.shape[1:3]
    local_len = chunk_tiles * tile_len
    kmax, ntiles = lists_ref.shape[1:]
    factor = HD ** (-0.5) * math.log2(math.e)
    valid = [min(owners, heads - slot * owners) for slot in range(slots)]
    half = owners // 2
    chip, core = lax.div(rank, 2), lax.rem(rank, 2)

    def guarded(slot, member_rank, body):
        if valid[slot] == owners:
            body()
        else:
            pl.when(member_rank < valid[slot])(body)

    def columns(slot, member_rank):
        return pl.ds(pl.multiple_of((slot * owners + member_rank) * HD, HD), HD)

    def rows(member_rank):
        return pl.ds(pl.multiple_of(member_rank * local_len, local_len), local_len)

    def tiles(member_rank):
        return pl.ds(member_rank * chunk_tiles, chunk_tiles)

    def flipped(index, distance):
        other = 0
        bit = 1
        while bit < half:
            other = other + bit * lax.rem(lax.div(index, bit) + lax.div(distance, bit), 2)
            bit *= 2
        return other

    def peer(step):
        return 2 * flipped(chip, lax.rem(step, half)) + lax.rem(core + lax.div(step, half), 2)

    def q_copy(slot, target, source):
        return pltpu.make_async_remote_copy(
            src_ref=fields_ref.at[0, :, :, columns(slot, target)],
            dst_ref=queries[slot].at[tiles(source)],
            send_sem=q_send.at[slot, target],
            recv_sem=q_recv.at[slot, source],
            device_id=(section, target),
            device_id_type=MESH,
        )

    def kv_copy(slot, target, source):
        return pltpu.make_async_remote_copy(
            src_ref=fields_ref.at[pl.ds(1, 2), :, :, columns(slot, target)],
            dst_ref=pairs[slot].at[:, tiles(source)],
            send_sem=kv_send.at[slot, target],
            recv_sem=kv_recv.at[slot, source],
            device_id=(section, target),
            device_id_type=MESH,
        )

    def own_q_copy(slot):
        return pltpu.make_async_copy(
            fields_ref.at[0, :, :, columns(slot, rank)],
            queries[slot].at[tiles(rank)],
            own_sem.at[slot, 0],
        )

    def own_kv_copy(slot):
        return pltpu.make_async_copy(
            fields_ref.at[pl.ds(1, 2), :, :, columns(slot, rank)],
            pairs[slot].at[:, tiles(rank)],
            own_sem.at[slot, 1],
        )

    def out_copy(slot, target, source):
        return pltpu.make_async_remote_copy(
            src_ref=staged[slot].at[rows(target), :],
            dst_ref=out_ref.at[:, columns(slot, source)],
            send_sem=out_send.at[slot, target],
            recv_sem=out_recv.at[slot, source],
            device_id=(after, target),
            device_id_type=MESH,
        )

    def each(first, last, body):
        def step(i, carry):
            body(peer(i))
            return carry

        lax.fori_loop(first, last, step, 0)

    def to_core(slot, side, body):
        def one(target):
            guarded(slot, target, lambda: body(target))

        pl.when(core != side)(lambda: one(2 * chip + side))

        def step(distance, carry):
            one(2 * flipped(chip, distance) + side)
            return carry

        lax.fori_loop(1, half, step, 0)

    def sent_then(copy, slot, side):
        def one(target):
            guarded(slot, target, lambda: copy(slot, target, rank).wait_send())
            if slot + 1 < slots:
                guarded(slot + 1, target, lambda: copy(slot + 1, target, rank).start())

        pl.when(core != side)(lambda: one(2 * chip + side))

        def step(distance, carry):
            one(2 * flipped(chip, distance) + side)
            return carry

        lax.fori_loop(1, half, step, 0)

    usable[0] = jnp.zeros((tile_len, HD), jnp.bfloat16)
    usable[1] = jnp.ones((tile_len, HD), jnp.bfloat16)
    for slot in range(slots):
        pairs[slot][:, ntiles] = jnp.zeros((2, tile_len, HD), jnp.bfloat16)

    barrier = pltpu.get_barrier_semaphore()

    def greet(place):
        def one(target):
            pl.semaphore_signal(barrier, inc=1, device_id=(place, target), device_id_type=MESH)

        return one

    each(1, owners, greet(section))
    each(0, owners, greet(before))

    def start_own(slot):
        own_q_copy(slot).start()
        own_kv_copy(slot).start()

    for slot in range(slots):
        guarded(slot, rank, functools.partial(start_own, slot))
    pl.semaphore_wait(barrier, 2 * owners - 1)

    for side in range(2):
        to_core(0, side, lambda target: kv_copy(0, target, rank).start())
        to_core(0, side, lambda target: q_copy(0, target, rank).start())

    for slot in range(slots):
        def gather_pairs(slot=slot):
            own_q_copy(slot).wait()
            own_kv_copy(slot).wait()
            each(1, owners, lambda source: kv_copy(slot, rank, source).wait_recv())

        def attend_chunks(first, last, slot=slot):
            head = slot * owners + rank
            kind = class_ref[head]
            gate_part = gate_ref[:, pl.ds(pl.multiple_of(head * HD, HD), HD)].astype(jnp.float32)

            def attend_tile(tile):
                here = pl.ds(pl.multiple_of(tile * tile_len, tile_len), tile_len)
                count = counts_ref[head, tile]
                places, fillers, flags = [tile], [tile], [1]
                for j in range(1, kmax):
                    listed = lists_ref[0, j, tile] + kind * (
                        lists_ref[1, j, tile] - lists_ref[0, j, tile]
                    )
                    places.append(jnp.where(j < count, listed, tile))
                    fillers.append(jnp.where(j < count, listed, ntiles))
                    flags.append(jnp.where(j < count, 1, 0))
                keys = jnp.concatenate([pairs[slot][0, place] for place in places], axis=0)
                values = jnp.concatenate([pairs[slot][1, place] for place in fillers], axis=0)
                marks = jnp.concatenate([usable[flag] for flag in flags], axis=0)
                values = jnp.concatenate([values, marks], axis=1)
                scores = lax.dot_general(
                    queries[slot][tile],
                    keys,
                    (((1,), (1,)), ((), ())),
                    preferred_element_type=jnp.float32,
                )
                highest = jnp.max(scores, axis=-1, keepdims=True)
                raised = jnp.exp2((scores - highest) * factor).astype(jnp.bfloat16)
                mixed = jnp.dot(raised, values, preferred_element_type=jnp.float32)
                mixed = mixed[:, :HD] / mixed[:, HD:]
                mixed = mixed.astype(jnp.bfloat16).astype(jnp.float32)
                staged[slot][here, :] = (gate_part * mixed).astype(jnp.bfloat16)

            def attend_chunk(step, carry):
                target = peer(step)

                @pl.when(step > 0)
                def _():
                    q_copy(slot, rank, target).wait_recv()

                def attend_two(i, inner):
                    attend_tile(target * chunk_tiles + 2 * i)
                    attend_tile(target * chunk_tiles + 2 * i + 1)
                    return inner

                if chunk_tiles % 2 == 0:
                    lax.fori_loop(0, chunk_tiles // 2, attend_two, 0)
                else:
                    for i in range(chunk_tiles):
                        attend_tile(target * chunk_tiles + i)
                out_copy(slot, target, rank).start()
                return carry

            lax.fori_loop(first, last, attend_chunk, 0)

        def attend_slot(slot=slot, attend_chunks=attend_chunks, gather_pairs=gather_pairs):
            gather_pairs()
            attend_chunks(0, owners)

        for side in range(2):
            for copy in (kv_copy, q_copy):
                sent_then(copy, slot, side)

            @pl.when(core == side)
            def _(slot=slot, attend_slot=attend_slot):
                guarded(slot, rank, attend_slot)

    for slot in range(slots):

        def finish_send(slot=slot):
            each(0, owners, lambda target: out_copy(slot, target, rank).wait_send())

        guarded(slot, rank, finish_send)

        def finish_recv(source, carry, slot=slot):
            out_copy(slot, rank, source).wait_recv()
            return carry

        lax.fori_loop(0, valid[slot], finish_recv, 0)


def local(sections, owners, projected, gate, head_class, tile_lists, tile_counts):
    local_len, width = projected.shape[2:]
    heads = width // HD
    slots = -(-heads // owners)
    tokens = owners * local_len
    ntiles, kmax = tile_lists.shape[1:]
    tile_len = tokens // ntiles
    fields = projected.reshape(3, local_len // tile_len, tile_len, width)
    flops = 4 * slots * ntiles * tile_len * kmax * tile_len * HD
    smem = pl.BlockSpec(memory_space=pltpu.SMEM)
    out = pl.pallas_call(
        functools.partial(relay_kernel, heads, owners, sections, slots),
        out_shape=jax.ShapeDtypeStruct((local_len, width), jnp.bfloat16),
        in_specs=[smem, smem, smem, pl.BlockSpec(memory_space=pltpu.VMEM), pl.BlockSpec(memory_space=pl.ANY)],
        out_specs=pl.BlockSpec(memory_space=pl.ANY),
        scratch_shapes=[pltpu.VMEM((ntiles, tile_len, HD), jnp.bfloat16)] * slots
        + [pltpu.VMEM((2, ntiles + 1, tile_len, HD), jnp.bfloat16)] * slots
        + [pltpu.VMEM((tokens, HD), jnp.bfloat16)] * slots
        + [pltpu.VMEM((2, tile_len, HD), jnp.bfloat16)]
        + [
            pltpu.SemaphoreType.DMA((slots, 2)),
            pltpu.SemaphoreType.DMA((slots, owners)),
            pltpu.SemaphoreType.DMA((slots, owners)),
            pltpu.SemaphoreType.DMA((slots, owners)),
            pltpu.SemaphoreType.DMA((slots, owners)),
            pltpu.SemaphoreType.DMA((slots, owners)),
            pltpu.SemaphoreType.DMA((slots, owners)),
        ],
        compiler_params=pltpu.CompilerParams(
            collective_id=0, has_side_effects=True, vmem_limit_bytes=56 * 1024 * 1024
        ),
        cost_estimate=pl.CostEstimate(
            flops=flops, bytes_accessed=8 * local_len * width, transcendentals=flops // (4 * HD)
        ),
    )(head_class, tile_lists.transpose(0, 2, 1), tile_counts, gate, fields)
    return out[None]


def solution(mesh):
    placed = (P("section", None, "seq", None), P("section", None), P(), P(), P())
    return jax.shard_map(
        functools.partial(local, mesh.shape["section"], mesh.shape["seq"]),
        mesh=mesh,
        in_specs=placed,
        out_specs=P("section", "seq", None),
        check_vma=False,
    )
```

```python
import functools
import math

import jax
import jax.numpy as jnp
from jax import lax
from jax.experimental import pallas as pl
from jax.experimental.pallas import tpu as pltpu
from jax.sharding import PartitionSpec as P

HD = 128
MESH = pl.DeviceIdType.MESH


def relay_kernel(
    heads,
    owners,
    sections,
    slots,
    class_ref,
    lists_ref,
    counts_ref,
    gate_ref,
    fields_ref,
    out_ref,
    *scratch,
):
    queries = scratch[:slots]
    pairs = scratch[slots : 2 * slots]
    staged = scratch[2 * slots : 3 * slots]
    parcels, landed, own_sem, pack_sem, land_sem = scratch[3 * slots : 3 * slots + 5]
    q_send, q_recv, kv_send, kv_recv, out_send, out_recv = scratch[3 * slots + 5 :]
    section = lax.axis_index("section")
    rank = lax.axis_index("seq")
    after = lax.rem(section + 1, sections)
    before = lax.rem(section + sections - 1, sections)
    chunk_tiles, tile_len = fields_ref.shape[1:3]
    local_len = chunk_tiles * tile_len
    kmax = lists_ref.shape[1]
    factor = HD ** (-0.5) * math.log2(math.e)
    valid = [min(owners, heads - slot * owners) for slot in range(slots)]
    half = owners // 2

    def guarded(slot, member_rank, body):
        if valid[slot] == owners:
            body()
        else:
            pl.when(member_rank < valid[slot])(body)

    def columns(slot, member_rank):
        return pl.ds(pl.multiple_of((slot * owners + member_rank) * HD, HD), HD)

    def rows(member_rank):
        return pl.ds(pl.multiple_of(member_rank * local_len, local_len), local_len)

    def tiles(member_rank):
        return pl.ds(member_rank * chunk_tiles, chunk_tiles)

    def peer(step):
        distance = 2 * lax.rem(step, half) + lax.div(step, half)
        other = 0
        bit = 1
        while bit < owners:
            other = other + bit * lax.rem(lax.div(rank, bit) + lax.div(distance, bit), 2)
            bit *= 2
        return other

    def q_copy(slot, target, source):
        return pltpu.make_async_remote_copy(
            src_ref=parcels.at[slot * owners + target, 0],
            dst_ref=queries[slot].at[tiles(source)],
            send_sem=q_send.at[slot, target],
            recv_sem=q_recv.at[slot, source],
            device_id=(section, target),
            device_id_type=MESH,
        )

    def kv_copy(slot, target, source):
        return pltpu.make_async_remote_copy(
            src_ref=parcels.at[slot * owners + target, pl.ds(1, 2)],
            dst_ref=pairs[slot].at[:, tiles(source)],
            send_sem=kv_send.at[slot, target],
            recv_sem=kv_recv.at[slot, source],
            device_id=(section, target),
            device_id_type=MESH,
        )

    def pack_copy(slot, target):
        return pltpu.make_async_copy(
            fields_ref.at[:, :, :, columns(slot, target)],
            parcels.at[slot * owners + target],
            pack_sem.at[slot, target],
        )

    def land_copy(slot, source):
        return pltpu.make_async_copy(
            landed.at[slot * owners + source],
            out_ref.at[:, columns(slot, source)],
            land_sem.at[slot, source],
        )

    def own_q_copy(slot):
        return pltpu.make_async_copy(
            fields_ref.at[0, :, :, columns(slot, rank)],
            queries[slot].at[tiles(rank)],
            own_sem.at[slot, 0],
        )

    def own_kv_copy(slot):
        return pltpu.make_async_copy(
            fields_ref.at[pl.ds(1, 2), :, :, columns(slot, rank)],
            pairs[slot].at[:, tiles(rank)],
            own_sem.at[slot, 1],
        )

    def out_copy(slot, target, source):
        return pltpu.make_async_remote_copy(
            src_ref=staged[slot].at[rows(target), :],
            dst_ref=landed.at[slot * owners + source],
            send_sem=out_send.at[slot, target],
            recv_sem=out_recv.at[slot, source],
            device_id=(after, target),
            device_id_type=MESH,
        )

    def each(first, last, body):
        def step(i, carry):
            body(peer(i))
            return carry

        lax.fori_loop(first, last, step, 0)

    def to_peers(slot, first, last, body):
        each(first, last, lambda target: guarded(slot, target, lambda: body(target)))

    barrier = pltpu.get_barrier_semaphore()

    def greet(place):
        def one(target):
            pl.semaphore_signal(barrier, inc=1, device_id=(place, target), device_id_type=MESH)

        return one

    each(1, owners, greet(section))
    each(0, owners, greet(before))

    def start_own(slot):
        own_q_copy(slot).start()
        own_kv_copy(slot).start()

    for slot in range(slots):
        to_peers(slot, 1, owners, lambda target: pack_copy(slot, target).start())
        guarded(slot, rank, functools.partial(start_own, slot))
    pl.semaphore_wait(barrier, 2 * owners - 1)

    def kv_start(slot, target):
        pack_copy(slot, target).wait()
        kv_copy(slot, target, rank).start()

    to_peers(0, 1, owners, functools.partial(kv_start, 0))
    if slots > 1:
        to_peers(0, 1, owners, lambda target: q_copy(0, target, rank).start())

    for slot in range(slots):
        final = slot == slots - 1

        def kv_sent(target, slot=slot):
            kv_copy(slot, target, rank).wait_send()

        def q_start(target, slot=slot):
            q_copy(slot, target, rank).start()

        def q_sent(target, slot=slot):
            q_copy(slot, target, rank).wait_send()

        def gather_pairs(slot=slot):
            own_q_copy(slot).wait()
            own_kv_copy(slot).wait()
            each(1, owners, lambda source: kv_copy(slot, rank, source).wait_recv())

        def attend_chunks(first, last, slot=slot):
            head = slot * owners + rank
            kind = class_ref[head]
            gate_part = gate_ref[:, pl.ds(pl.multiple_of(head * HD, HD), HD)].astype(jnp.float32)

            def attend_tile(tile):
                here = pl.ds(pl.multiple_of(tile * tile_len, tile_len), tile_len)
                places = [
                    lists_ref[0, j, tile] + kind * (lists_ref[1, j, tile] - lists_ref[0, j, tile])
                    for j in range(kmax)
                ]
                keys = jnp.concatenate([pairs[slot][0, place] for place in places], axis=0)
                values = jnp.concatenate([pairs[slot][1, place] for place in places], axis=0)
                scores = lax.dot_general(
                    queries[slot][tile],
                    keys,
                    (((1,), (1,)), ((), ())),
                    preferred_element_type=jnp.float32,
                )
                index = lax.broadcasted_iota(jnp.int32, scores.shape, 1)
                scores = jnp.where(index < counts_ref[head, tile] * tile_len, scores, -jnp.inf)
                highest = jnp.max(scores, axis=-1, keepdims=True)
                raised = jnp.exp2((scores - highest) * factor)
                total = jnp.sum(raised, axis=-1, keepdims=True)
                weights = (raised * (1.0 / total)).astype(jnp.bfloat16)
                mixed = jnp.dot(weights, values, preferred_element_type=jnp.float32)
                mixed = mixed.astype(jnp.bfloat16).astype(jnp.float32)
                staged[slot][here, :] = (gate_part * mixed).astype(jnp.bfloat16)

            def attend_chunk(step, carry):
                target = peer(step)

                @pl.when(step > 0)
                def _():
                    q_copy(slot, rank, target).wait_recv()

                def attend_two(i, inner):
                    attend_tile(target * chunk_tiles + 2 * i)
                    attend_tile(target * chunk_tiles + 2 * i + 1)
                    return inner

                if chunk_tiles % 2 == 0:
                    lax.fori_loop(0, chunk_tiles // 2, attend_two, 0)
                else:
                    for i in range(chunk_tiles):
                        attend_tile(target * chunk_tiles + i)
                out_copy(slot, target, rank).start()
                return carry

            lax.fori_loop(first, last, attend_chunk, 0)

        if not final:

            def kv_next(target, slot=slot):
                guarded(slot, target, lambda: kv_copy(slot, target, rank).wait_send())
                guarded(slot + 1, target, lambda: kv_start(slot + 1, target))

            each(1, owners, kv_next)
            guarded(slot, rank, gather_pairs)
            guarded(slot, rank, functools.partial(attend_chunks, 0, owners))
            to_peers(slot, 1, owners, q_sent)
            if slot + 1 < slots - 1:
                to_peers(
                    slot + 1, 1, owners, lambda target: q_copy(slot + 1, target, rank).start()
                )
        else:

            def q_after_kv(target):
                kv_sent(target)
                q_start(target)

            to_peers(slot, 1, half, q_after_kv)
            guarded(slot, rank, gather_pairs)
            guarded(slot, rank, functools.partial(attend_chunks, 0, 1))
            to_peers(slot, 1, half, q_sent)
            to_peers(slot, half, owners, q_after_kv)
            guarded(slot, rank, functools.partial(attend_chunks, 1, owners))
            to_peers(slot, half, owners, q_sent)

    for slot in range(slots):

        def finish_recv(source, carry, slot=slot):
            out_copy(slot, rank, source).wait_recv()
            land_copy(slot, source).start()
            return carry

        lax.fori_loop(0, valid[slot], finish_recv, 0)

    for slot in range(slots):

        def finish_send(slot=slot):
            each(0, owners, lambda target: out_copy(slot, target, rank).wait_send())

        def finish_land(source, carry, slot=slot):
            land_copy(slot, source).wait()
            return carry

        guarded(slot, rank, finish_send)
        lax.fori_loop(0, valid[slot], finish_land, 0)


def local(sections, owners, projected, gate, head_class, tile_lists, tile_counts):
    local_len, width = projected.shape[2:]
    heads = width // HD
    slots = -(-heads // owners)
    tokens = owners * local_len
    ntiles, kmax = tile_lists.shape[1:]
    tile_len = tokens // ntiles
    fields = projected.reshape(3, local_len // tile_len, tile_len, width)
    flops = 4 * slots * ntiles * tile_len * kmax * tile_len * HD
    smem = pl.BlockSpec(memory_space=pltpu.SMEM)
    out = pl.pallas_call(
        functools.partial(relay_kernel, heads, owners, sections, slots),
        out_shape=jax.ShapeDtypeStruct((local_len, width), jnp.bfloat16),
        in_specs=[smem, smem, smem, pl.BlockSpec(memory_space=pltpu.VMEM), pl.BlockSpec(memory_space=pl.ANY)],
        out_specs=pl.BlockSpec(memory_space=pl.ANY),
        scratch_shapes=[pltpu.VMEM((ntiles, tile_len, HD), jnp.bfloat16)] * slots
        + [pltpu.VMEM((2, ntiles, tile_len, HD), jnp.bfloat16)] * slots
        + [pltpu.VMEM((tokens, HD), jnp.bfloat16)] * slots
        + [
            pltpu.VMEM((slots * owners, 3, local_len // tile_len, tile_len, HD), jnp.bfloat16),
            pltpu.VMEM((slots * owners, local_len, HD), jnp.bfloat16),
            pltpu.SemaphoreType.DMA((slots, 2)),
            pltpu.SemaphoreType.DMA((slots, owners)),
            pltpu.SemaphoreType.DMA((slots, owners)),
            pltpu.SemaphoreType.DMA((slots, owners)),
            pltpu.SemaphoreType.DMA((slots, owners)),
            pltpu.SemaphoreType.DMA((slots, owners)),
            pltpu.SemaphoreType.DMA((slots, owners)),
            pltpu.SemaphoreType.DMA((slots, owners)),
            pltpu.SemaphoreType.DMA((slots, owners)),
        ],
        compiler_params=pltpu.CompilerParams(
            collective_id=0, has_side_effects=True, vmem_limit_bytes=56 * 1024 * 1024
        ),
        cost_estimate=pl.CostEstimate(
            flops=flops, bytes_accessed=8 * local_len * width, transcendentals=flops // (4 * HD)
        ),
    )(head_class, tile_lists.transpose(0, 2, 1), tile_counts, gate, fields)
    return out[None]


def solution(mesh):
    placed = (P("section", None, "seq", None), P("section", None), P(), P(), P())
    return jax.shard_map(
        functools.partial(local, mesh.shape["section"], mesh.shape["seq"]),
        mesh=mesh,
        in_specs=placed,
        out_specs=P("section", "seq", None),
        check_vma=False,
    )
```
